256 devices in a mesh: rep: 16 (over x_hi, z), fsdp: 16 (over x_lo, y, core).
Axes of the slice: x: 4 (x_hi: 2, x_lo: 2; x = x_hi * 2 + x_lo), y: 4, z: 8, core: 2. Of those that a mesh axis runs over, the one named last changes fastest.
Arguments:
- activations: bfloat16 [98304, 8192], P(('rep', 'fsdp')), may hold values from -6 to 6
- cotangent: bfloat16 [98304, 512], P(('rep', 'fsdp')), may hold values from -0.078125 to 0.078125
- momentum: float32 [16, 8192, 512], P('rep', 'fsdp'), may hold values from -6 to 6
- params: float32 [8192, 512], P('fsdp'), may hold values from -6 to 6
- band: int32 [128, 8, 32], P('fsdp'), may hold values from 0 to 975, as said below
Outputs:
- new_weights: bfloat16 [8192, 512], replicated
- new_momentum: float32 [16, 8192, 512], P('rep', 'fsdp')
The draws below stay inside these ranges and needn't reach their ends.
Inputs may be any that keep to these rules, and one draw needn't show every extreme that they name: `band`: in every span the 32 positions are distinct, lie in rows 0 to 15 and columns 0 to 15 of the span's coefficients, and include 0 and 975.
All inputs are finite; a program needn't handle non-finite values.
Results may differ from the reference program's by a relative error of at most 0.001.
Values may be sent and summed in bfloat16 or wider, within the bound.
A program may use at most 128 MiB of HBM per device.

```python
import jax
import jax.numpy as jnp
from jax import lax

D = 8192
COLS = 512
TOK_DEV = 384
K = 32
TOKENS = 98304
N_REP = 16
N_FSDP = 16


def draw_band(key, part):
    key = jax.random.fold_in(key, 7)
    span_count = D // 64 * (COLS // 64)
    key_list = jax.random.split(key, span_count)
    picked = jax.vmap(lambda single: jax.random.permutation(single, 254)[:K - 2] + 1)(key_list)
    extremes = jnp.broadcast_to(jnp.array([0, 255], jnp.int32), (span_count, 2))
    corner = jnp.concatenate([extremes, picked.astype(jnp.int32)], axis=1)
    table = corner // 16 * 64 + corner % 16
    return table.astype(jnp.int32).reshape(D // 64, COLS // 64, K)


def block_levels(stream_key, extent, pieces, smallest, high):
    def one(dim, parts):
        steps = jax.random.uniform(jax.random.fold_in(jax.random.fold_in(stream_key, 6), dim), (parts,), jnp.float32, smallest / len(pieces), high / len(pieces))
        return jnp.repeat(jnp.exp(steps), extent[dim] // parts).reshape((-1,) + (1,) * (len(extent) - dim - 1))

    loudness = one(*pieces[0])
    for cut in pieces[1:]:
        loudness = loudness * one(*cut)
    return loudness


def noise(rng, extent, deviation, reach, pieces=(), kind=jnp.bfloat16):
    drawn = deviation * jax.random.normal(rng, extent, jnp.float32)
    if pieces:
        drawn = drawn * block_levels(rng, extent, pieces, -0.22, 0.18)
    return jnp.clip(drawn, -reach, reach).astype(kind)


def setup_inputs(seed: int = 0) -> dict:
    seeds = jax.random.split(jax.random.key(seed), 6)
    activations = noise(seeds[0], (TOKENS, D), 1.0, 6.0, ((0, 256),))
    cotangent = noise(seeds[1], (TOKENS, COLS), (TOK_DEV * N_FSDP) ** -0.5, 0.078125, ((0, 256),))
    momentum = noise(seeds[2], (N_REP, D, COLS), 1.0, 6.0, ((0, 16), (1, 16)), jnp.float32)
    params = noise(seeds[3], (D, COLS), 1.0, 6.0, ((0, 16),), jnp.float32)
    band = draw_band(jax.random.fold_in(seeds[5], 71), 0)
    return {"activations": activations, "cotangent": cotangent, "momentum": momentum, "params": params, "band": band}


def dct_matrix():
    frequency = jnp.arange(64, dtype=jnp.float32)[:, None]
    position = jnp.arange(64, dtype=jnp.float32)[None, :]
    scaling = jnp.where(frequency == 0, jnp.sqrt(1.0 / 64.0), jnp.sqrt(2.0 / 64.0))
    return (scaling * jnp.cos(jnp.pi * (2.0 * position + 1.0) * frequency / 128.0)).astype(jnp.float32)

def forward_spans(field, matrix):
    spans = field.reshape(D // 64, 64, COLS // 64, 64)
    coefs = jnp.einsum('ki,aibj,lj->abkl', matrix, spans, matrix, precision=lax.Precision.HIGHEST)
    return coefs.reshape(D // 64, COLS // 64, 4096)

def inverse_spans(sparse, matrix):
    spans = sparse.reshape(D // 64, COLS // 64, 64, 64)
    field = jnp.einsum('ki,abkl,lj->aibj', matrix, spans, matrix, precision=lax.Precision.HIGHEST)
    return field.reshape(D, COLS)

def spread(values, band):
    row_index = jnp.arange(D // 64, dtype=jnp.int32)[:, None, None]
    col_index = jnp.arange(COLS // 64, dtype=jnp.int32)[None, :, None]
    empty = jnp.zeros((D // 64, COLS // 64, 4096), jnp.float32)
    return empty.at[row_index, col_index, band].add(values)

def reference(activations, cotangent, momentum, params, band):
    matrix = dct_matrix()
    grouped_acts = activations.reshape(N_REP, TOK_DEV * N_FSDP, D)
    grouped_cots = cotangent.reshape(N_REP, TOK_DEV * N_FSDP, COLS)

    def replica(items):
        act_block, cot_block, moment = items
        gradient = jnp.dot(act_block.T, cot_block, preferred_element_type=jnp.float32)
        blended = 0.9 * moment + gradient
        coefs = forward_spans(blended, matrix)
        chosen = jnp.take_along_axis(coefs, band, axis=2)
        residual = blended - inverse_spans(spread(chosen, band), matrix)
        return (chosen, residual)
    chosen_all, new_momentum = lax.map(replica, (grouped_acts, grouped_cots, momentum))
    mean_band = lax.optimization_barrier(jnp.sum(chosen_all, axis=0)) / N_REP
    update = inverse_spans(spread(mean_band, band), matrix)
    new_weights = (params - 32.0 * update).astype(jnp.bfloat16)
    return (new_weights, new_momentum)
```

```python
import jax
import jax.numpy as jnp
import numpy as np
from jax import lax
from jax.experimental import pallas as pl
from jax.experimental.pallas import tpu as pltpu
from jax.sharding import PartitionSpec as P

MESH = pl.DeviceIdType.MESH
HIGHEST = lax.Precision.HIGHEST
beta_decay = 0.9
step_size = 32.0
N_REP = 16
ROWS = 512
COLS = 512
TOK = 384
QUARTER = 128
PACKED = 4 * QUARTER + 16
CODE = 64.0
FULL = 32000.0
X_LO_ROWS = 128

ORDER = [(1, 2), (0, 2), (1, 1), (1, 3), (0, 1), (0, 3), (1, 0), (0, 0)]


def band_matrix():
    frequency = np.arange(16)[:, None]
    position = np.arange(64)[None, :]
    scaling = np.where(frequency == 0, np.sqrt(1.0 / 64.0), np.sqrt(2.0 / 64.0))
    table = scaling * np.cos(np.pi * (2.0 * position + 1.0) * frequency / 128.0)
    return np.kron(np.eye(8), table).astype(np.float32)


def dot_last(a, b, precision=HIGHEST):
    return lax.dot_general(
        a, b, (((1,), (1,)), ((), ())), precision=precision, preferred_element_type=jnp.float32
    )


def dot(a, b, precision=HIGHEST):
    return lax.dot_general(
        a, b, (((1,), (0,)), ((), ())), precision=precision, preferred_element_type=jnp.float32
    )


def halves(x):
    high = x.astype(jnp.bfloat16)
    return high, (x - high.astype(jnp.float32)).astype(jnp.bfloat16)


MESSAGES = (
    [("x1", dy, q) for dy in (2, 1, 3, 0) for q in (0, 1)]
    + [(ring, part) for ring in ("b1", "b0", "a0") for part in ("p1lo", "p1hi", "p2hi", "p2lo", "p3lo", "p3hi")]
    + [("x3", q) for q in (2, 3)]
)
SLOT = {key: i for i, key in enumerate(MESSAGES)}
GATHERS = (
    [("core", dx, dy, part) for dx in (0, 1) for dy in range(4) for part in (0, 1)]
    + [("y+",), ("y-",), ("y++",), ("y--",)]
    + [("xlo", dy) for dy in range(4)]
    + [("xhi", dy) for dy in range(4)]
)
GATHER = {key: i for i, key in enumerate(GATHERS)}


def kernel(
    act_hbm, cot_hbm, mom_hbm, par_hbm, band_hbm, f_hbm, ft_hbm,
    new_w, new_m,
    act, cot, mom, par, band, fm, ftm, weights, g, head, base, mask, out_q, in_q,
    corner_out, corner_in, csum, slice_in, mean,
    local_sem, act_sem, act_send, act_recv, cot_send, cot_recv, q_send, q_recv, c_send, c_recv,
    r_send, r_recv, m_send, m_recv, w_send, w_recv,
):
    rep, fsdp = lax.axis_index("rep"), lax.axis_index("fsdp")
    x_hi, z = rep // 8, lax.rem(rep, 8)
    x_lo, y, core = fsdp // 8, lax.rem(fsdp // 2, 4), lax.rem(fsdp, 2)

    def chunk(dx, dy):
        return lax.rem(x_lo + dx, 2) * 4 + lax.rem(y + dy, 4)

    def shard(dx, dy, dc=0):
        return chunk(dx, dy) * 2 + lax.rem(core + dc, 2)

    def peer(dx, dy, dc=0):
        return (rep, shard(dx, dy, dc))

    def rep_peer(k):
        return (lax.rem(rep + k, N_REP), fsdp)

    x_hi_peer = (lax.rem(x_hi + 1, 2) * 8 + z, shard(1, 0))
    x_peer, up, down, sibling = peer(1, 0), peer(0, 1), peer(0, 3), peer(0, 0, 1)

    mine = [pltpu.make_async_copy(cot_hbm, cot.at[pl.ds(0, TOK)], local_sem.at[0])]
    mine[0].start()

    def act_local(dx, dy):
        i = chunk(dx, dy)
        column = pl.multiple_of((i * 2 + core) * ROWS, ROWS)
        return pltpu.make_async_copy(
            act_hbm.at[:, pl.ds(column, ROWS)], act.at[i, pl.ds(0, TOK)], act_sem.at[i]
        )

    for dx, dy in ORDER:
        act_local(dx, dy).start()
    for i, (src, dst) in enumerate(
        [(mom_hbm.at[0], mom), (par_hbm, par), (band_hbm, band), (f_hbm, fm), (ft_hbm, ftm)]
    ):
        mine.append(pltpu.make_async_copy(src, dst, local_sem.at[i + 1]))
        mine[-1].start()

    barrier = pltpu.get_barrier_semaphore()
    greeted = [sibling, x_hi_peer]
    greeted += [peer(dx, dy) for dx, dy in ORDER if (dx, dy) != (0, 0)]
    greeted += [rep_peer(k) for k in range(1, N_REP)]
    for other in greeted:
        pl.semaphore_signal(barrier, inc=1, device_id=other, device_id_type=MESH)
    pl.semaphore_wait(barrier, len(greeted))

    cot_copy = pltpu.make_async_remote_copy(
        src_ref=cot_hbm, dst_ref=cot.at[pl.ds(TOK, TOK)], send_sem=cot_send, recv_sem=cot_recv,
        device_id=sibling, device_id_type=MESH,
    )
    cot_copy.start()

    def act_copy(dx, dy):
        i = chunk(dx, dy)
        column = pl.multiple_of((i * 2 + 1 - core) * ROWS, ROWS)
        return pltpu.make_async_remote_copy(
            src_ref=act_hbm.at[:, pl.ds(column, ROWS)], dst_ref=act.at[i, pl.ds(TOK, TOK)],
            send_sem=act_send.at[i], recv_sem=act_recv.at[i], device_id=sibling, device_id_type=MESH,
        )

    for dx, dy in ORDER:
        act_copy(dx, dy).start()

    for copy in mine:
        copy.wait()
    cot_copy.wait()
    turned = cot[...].astype(jnp.float32).T.astype(jnp.bfloat16)
    weights[pl.ds(0, COLS), :] = turned
    f_high, f_low = halves(fm[...])
    low = dot(f_high, turned, None) + dot(f_low, turned, None)
    low_high, low_low = halves(low)
    weights[pl.ds(COLS, 128), :] = low_high
    weights[pl.ds(COLS + 128, 128), :] = low_low

    def rows_of(q, r, p):
        return pl.ds(pl.multiple_of(q * QUARTER + r * 32, 32), 32), pl.ds(p * 128, 128)

    def peak_of(i, q):
        def body(r, peak):
            for p in range(4):
                rows, lanes = rows_of(q, r, p)
                v = jnp.abs(g[i, rows, lanes])
                peak = jnp.maximum(peak, jnp.max(v.reshape(4, 8, 128), axis=0))
            return peak

        return lax.fori_loop(0, QUARTER // 32, body, jnp.zeros((8, 128), jnp.float32))

    def unpack(key, r, p):
        slot = SLOT[key]
        rows = pl.ds(pl.multiple_of(p * QUARTER + r * 32, 32), 32)
        return in_q[slot, rows, :].astype(jnp.int32).astype(jnp.float32)

    def scale_of(code):
        return jnp.exp(code.astype(jnp.int32).astype(jnp.float32) * (1.0 / CODE)) * (1.0 / FULL)

    def received_scale(key):
        code = in_q[SLOT[key], pl.ds(4 * QUARTER, 16), :]
        return scale_of(code)[0:1]

    def add_received(i, q, keys):
        scales = [received_scale(key) for key in keys]

        def body(r, peak):
            for p in range(4):
                rows, lanes = rows_of(q, r, p)
                v = g[i, rows, lanes]
                for key, scale in zip(keys, scales, strict=True):
                    v = v + unpack(key, r, p) * scale
                g[i, rows, lanes] = v
                peak = jnp.maximum(peak, jnp.max(jnp.abs(v).reshape(4, 8, 128), axis=0))
            return peak

        return lax.fori_loop(0, QUARTER // 32, body, jnp.zeros((8, 128), jnp.float32))

    def message(key, target):
        slot = SLOT[key]
        return pltpu.make_async_remote_copy(
            src_ref=out_q.at[slot], dst_ref=in_q.at[slot], send_sem=q_send.at[slot],
            recv_sem=q_recv.at[slot], device_id=target, device_id_type=MESH,
        )

    target_of = {"p1lo": up, "p1hi": down, "p2hi": up, "p2lo": down, "p3lo": up, "p3hi": down}

    def message_of(key):
        return message(key, x_peer if key[0] in ("x1", "x3") else target_of[key[1]])

    def send(key, i, q, peak):
        slot = SLOT[key]
        peak = jnp.max(peak, axis=0, keepdims=True)
        code = jnp.ceil(jnp.log(jnp.maximum(peak, 1e-30)) * CODE) + 1.0
        code = jnp.broadcast_to(code, (16, 128)).astype(jnp.int32).astype(jnp.int16)
        out_q[slot, pl.ds(4 * QUARTER, 16), :] = code
        inverse = 1.0 / scale_of(code)[0:1]

        def body(r, carry):
            for p in range(4):
                rows, lanes = rows_of(q, r, p)
                v = jnp.round(g[i, rows, lanes] * inverse).astype(jnp.int32).astype(jnp.int16)
                out_q[slot, pl.ds(pl.multiple_of(p * QUARTER + r * 32, 32), 32), :] = v
            return carry

        lax.fori_loop(0, QUARTER // 32, body, 0)
        message_of(key).start()

    def arrived(*keys):
        for key in keys:
            message_of(key).wait_recv()

    def corner_copy(dx, dy):
        k = dx * 4 + dy
        return pltpu.make_async_remote_copy(
            src_ref=corner_out.at[k], dst_ref=corner_in.at[k], send_sem=c_send.at[k],
            recv_sem=c_recv.at[k], device_id=peer(dx, dy), device_id_type=MESH,
        )

    for dx, dy in ORDER:
        i = chunk(dx, dy)
        act_local(dx, dy).wait()
        act_copy(dx, dy).wait()

        def product(n, carry, i=i):
            lanes = pl.ds(pl.multiple_of(n * 256, 256), 256)
            both = dot(weights[...], act[i, :, lanes], None)
            g[i, :, lanes] = both[:COLS]
            head[:, lanes] = both[COLS : COLS + 128] + both[COLS + 128 :]
            return carry

        lax.fori_loop(0, ROWS // 256, product, 0)
        corner_out[dx * 4 + dy] = dot_last(head[...], fm[...])
        if (dx, dy) != (0, 0):
            corner_copy(dx, dy).start()
        sends = []
        if dx == 1:
            sends += [(("x1", dy, q), q) for q in (0, 1)]
        ring = "b1" if dx else "b0"
        sends += {2: [((ring, "p1lo"), 2), ((ring, "p1hi"), 3)], 1: [((ring, "p2hi"), 3)], 3: [((ring, "p2lo"), 2)], 0: []}[dy]
        for key, q in sends:
            send(key, i, q, peak_of(i, q))

    lane = lax.broadcasted_iota(jnp.int32, (8, 128), 1)
    pick = jnp.where(lane // 16 == lax.broadcasted_iota(jnp.int32, (8, 128), 0), 1.0, 0.0)
    offset = (lax.rem(lax.broadcasted_iota(jnp.int32, (32, 128), 1), 16) * 64).astype(jnp.float32)
    column = lax.broadcasted_iota(jnp.int32, (16, 32, 128), 0).astype(jnp.float32)
    for b in range(8):
        places = band[:, b, :].astype(jnp.float32)
        spread = lax.dot_general(
            places, pick, (((0,), (0,)), ((), ())), precision=HIGHEST, preferred_element_type=jnp.float32
        )
        hit = jnp.where((spread - offset)[None] == column, 1.0, 0.0)
        mask[pl.ds(b * 16, 16), :] = jnp.max(hit, axis=1)
    momentum_low = dot_last(dot_last(fm[...], mom[...]), fm[...]) * beta_decay

    for ring, dx in (("b1", 1), ("b0", 0)):
        arrived((ring, "p1lo"))
        send((ring, "p3lo"), chunk(dx, 1), 2, add_received(chunk(dx, 1), 2, [(ring, "p1lo")]))
        arrived((ring, "p1hi"))
        send((ring, "p3hi"), chunk(dx, 3), 3, add_received(chunk(dx, 3), 3, [(ring, "p1hi")]))

    total = corner_out[0] + momentum_low
    for dx, dy in ORDER[:-1]:
        corner_copy(dx, dy).wait()
        total = total + corner_in[dx * 4 + dy]
    csum[...] = total

    def slice_rows(k):
        return pl.ds(pl.multiple_of(lax.rem(rep + k, N_REP) * 8, 8), 8)

    def slice_copy(k):
        return pltpu.make_async_remote_copy(
            src_ref=csum.at[slice_rows(k)], dst_ref=slice_in.at[k], send_sem=r_send.at[k],
            recv_sem=r_recv.at[k], device_id=rep_peer(k), device_id_type=MESH,
        )

    for k in range(1, N_REP):
        slice_copy(k).start()

    arrived(("x1", 2, 0))
    send(("a0", "p1lo"), chunk(0, 2), 0, add_received(chunk(0, 2), 0, [("x1", 2, 0)]))
    arrived(("x1", 2, 1))
    send(("a0", "p1hi"), chunk(0, 2), 1, add_received(chunk(0, 2), 1, [("x1", 2, 1)]))

    for k in range(1, N_REP):
        slice_copy(k).wait()
    part = csum[slice_rows(0), :]
    for k in range(1, N_REP):
        part = part + slice_in[k]
    mean[slice_rows(0), :] = part * (1.0 / N_REP)

    def mean_copy(k):
        return pltpu.make_async_remote_copy(
            src_ref=mean.at[slice_rows(0)], dst_ref=mean.at[slice_rows(0)], send_sem=m_send.at[k],
            recv_sem=m_recv.at[k], device_id=rep_peer(k), device_id_type=MESH,
        )

    for k in range(1, N_REP):
        mean_copy(k).start()

    arrived(("x1", 1, 1))
    send(("a0", "p2hi"), chunk(0, 1), 1, add_received(chunk(0, 1), 1, [("x1", 1, 1)]))
    arrived(("x1", 3, 0))
    send(("a0", "p2lo"), chunk(0, 3), 0, add_received(chunk(0, 3), 0, [("x1", 3, 0)]))

    def inverse(coefs):
        return dot(dot_last(ftm[...], coefs * mask[...]), fm[...])

    base[...] = beta_decay * mom[...] - inverse(csum[...])

    for k in range(1, N_REP):
        mean_copy(k).wait()

    def chunk_rows(dx, dy, dc=0, first=0, count=ROWS):
        return pl.ds(pl.multiple_of(shard(dx, dy, dc) * ROWS + first, 16), count)

    new_w[chunk_rows(0, 0), :] = (par[...] - step_size * inverse(mean[...])).astype(jnp.bfloat16)

    def gather_copy(key, rows, target):
        k = GATHER[key]
        return pltpu.make_async_remote_copy(
            src_ref=new_w.at[rows], dst_ref=new_w.at[rows], send_sem=w_send.at[k],
            recv_sem=w_recv.at[k], device_id=target, device_id_type=MESH,
        )

    copies = {}

    def gather(key, rows, target):
        copies[key] = gather_copy(key, rows, target)
        copies[key].start()

    gather(("y+",), chunk_rows(0, 0), up)
    gather(("y-",), chunk_rows(0, 0), down)

    def share(dy):
        gather(("xlo", dy), chunk_rows(0, dy, 0, 0, X_LO_ROWS), x_peer)
        gather(("xhi", dy), chunk_rows(0, dy, 0, X_LO_ROWS, ROWS - X_LO_ROWS), x_hi_peer)

    share(0)
    gather(("core", 0, 0, 0), chunk_rows(0, 0), sibling)

    arrived(("b1", "p2lo"), ("b1", "p3lo"))
    send(("x3", 2), chunk(1, 0), 2, add_received(chunk(1, 0), 2, [("b1", "p2lo"), ("b1", "p3lo")]))
    arrived(("b1", "p2hi"), ("b1", "p3hi"))
    send(("x3", 3), chunk(1, 0), 3, add_received(chunk(1, 0), 3, [("b1", "p2hi"), ("b1", "p3hi")]))

    arrived(("x1", 1, 0), ("a0", "p1lo"))
    send(("a0", "p3lo"), chunk(0, 1), 0, add_received(chunk(0, 1), 0, [("x1", 1, 0), ("a0", "p1lo")]))
    arrived(("x1", 3, 1), ("a0", "p1hi"))
    send(("a0", "p3hi"), chunk(0, 3), 1, add_received(chunk(0, 3), 1, [("x1", 3, 1), ("a0", "p1hi")]))

    copies[("y+",)].wait_recv()
    gather(("y++",), chunk_rows(0, 3, 0, 0, ROWS // 2), up)
    share(3)
    gather(("core", 0, 3, 0), chunk_rows(0, 3), sibling)
    copies[("y-",)].wait_recv()
    gather(("y--",), chunk_rows(0, 1, 0, ROWS // 2, ROWS // 2), down)
    share(1)
    gather(("core", 0, 1, 0), chunk_rows(0, 1), sibling)

    def finish(q, keys):
        arrived(*keys)
        add_received(chunk(0, 0), q, keys)
        lanes = pl.ds(q * QUARTER, QUARTER)
        new_m[0, :, lanes] = base[:, lanes] + g[chunk(0, 0), lanes, :].T

    finish(2, [("b0", "p2lo"), ("b0", "p3lo"), ("x3", 2)])
    finish(3, [("b0", "p2hi"), ("b0", "p3hi"), ("x3", 3)])

    copies[("y++",)].wait_recv()
    copies[("y--",)].wait_recv()
    share(2)
    gather(("core", 0, 2, 0), chunk_rows(0, 2), sibling)
    finish(0, [("x1", 0, 0), ("a0", "p2lo"), ("a0", "p3lo")])
    finish(1, [("x1", 0, 1), ("a0", "p2hi"), ("a0", "p3hi")])

    for dy in (0, 3, 1, 2):
        copies[("xlo", dy)].wait_recv()
        gather(("core", 1, dy, 0), chunk_rows(1, dy, 0, 0, X_LO_ROWS), sibling)
        copies[("xhi", dy)].wait_recv()
        gather(("core", 1, dy, 1), chunk_rows(1, dy, 0, X_LO_ROWS, ROWS - X_LO_ROWS), sibling)

    for key, copy in copies.items():
        copy.wait_send()
        if key[0] == "core":
            copy.wait_recv()
    for key in MESSAGES:
        message_of(key).wait_send()


def local(activations, cotangent, momentum, params, band, f, ft):
    any_space = pl.BlockSpec(memory_space=pl.ANY)
    i16, f32, bf16 = jnp.int16, jnp.float32, jnp.bfloat16
    dma = pltpu.SemaphoreType.DMA
    n = len(MESSAGES)
    return pl.pallas_call(
        kernel,
        out_shape=(
            pltpu.VMEM((16 * ROWS, COLS), bf16),
            pltpu.VMEM((1, ROWS, COLS), f32),
        ),
        in_specs=[any_space] * 7,
        out_specs=(pl.BlockSpec(memory_space=pltpu.VMEM), pl.BlockSpec(memory_space=pltpu.VMEM)),
        scratch_shapes=[
            pltpu.VMEM((8, 2 * TOK, ROWS), bf16),
            pltpu.VMEM((2 * TOK, COLS), bf16),
            pltpu.VMEM((ROWS, COLS), f32),
            pltpu.VMEM((ROWS, COLS), f32),
            pltpu.VMEM((8, 8, 32), jnp.int32),
            pltpu.VMEM((128, 512), f32),
            pltpu.VMEM((512, 128), f32),
            pltpu.VMEM((COLS + 256, 2 * TOK), bf16),
            pltpu.VMEM((8, COLS, ROWS), f32),
            pltpu.VMEM((128, ROWS), f32),
            pltpu.VMEM((ROWS, COLS), f32),
            pltpu.VMEM((128, 128), f32),
            pltpu.VMEM((n, PACKED, 128), i16),
            pltpu.VMEM((n, PACKED, 128), i16),
            pltpu.VMEM((8, 128, 128), f32),
            pltpu.VMEM((8, 128, 128), f32),
            pltpu.VMEM((128, 128), f32),
            pltpu.VMEM((N_REP, 8, 128), f32),
            pltpu.VMEM((128, 128), f32),
            dma((6,)), dma((8,)), dma((8,)), dma((8,)), dma, dma, dma((n,)), dma((n,)), dma((8,)), dma((8,)),
            dma((N_REP,)), dma((N_REP,)), dma((N_REP,)), dma((N_REP,)), dma((len(GATHERS),)), dma((len(GATHERS),)),
        ],
        compiler_params=pltpu.CompilerParams(
            collective_id=0, has_side_effects=True, vmem_limit_bytes=48 * 2**20
        ),
    )(activations, cotangent, momentum, params, band, f, ft)


def step(activations, cotangent, momentum, params, band):
    f = band_matrix()
    return local(activations, cotangent, momentum, params, band, jnp.asarray(f), jnp.asarray(f.T.copy()))


def solution(mesh):
    return jax.shard_map(
        step,
        mesh=mesh,
        in_specs=(
            P(("rep", "fsdp"), None),
            P(("rep", "fsdp"), None),
            P("rep", "fsdp", None),
            P("fsdp", None),
            P("fsdp", None, None),
        ),
        out_specs=(P(), P("rep", "fsdp", None)),
        check_vma=False,
    )
```

```python
import jax
import jax.numpy as jnp
import numpy as np
from jax import lax
from jax.experimental import pallas as pl
from jax.experimental.pallas import tpu as pltpu
from jax.sharding import PartitionSpec as P

MESH = pl.DeviceIdType.MESH
HIGHEST = lax.Precision.HIGHEST
beta_decay = 0.9
step_size = 32.0
N_REP = 16
ROWS = 512
COLS = 512
TOK = 384
QUARTER = 128
PACKED = 4 * QUARTER + 16
CODE = 64.0
FULL = 32000.0
KEPT = 64
PART = (ROWS - KEPT) // 4

ORDER = [(1, 2), (0, 2), (1, 1), (1, 3), (0, 1), (0, 3), (1, 0), (0, 0)]


def band_matrix():
    frequency = np.arange(16)[:, None]
    position = np.arange(64)[None, :]
    scaling = np.where(frequency == 0, np.sqrt(1.0 / 64.0), np.sqrt(2.0 / 64.0))
    table = scaling * np.cos(np.pi * (2.0 * position + 1.0) * frequency / 128.0)
    return np.kron(np.eye(8), table).astype(np.float32)


def dot_last(a, b, precision=HIGHEST):
    return lax.dot_general(
        a, b, (((1,), (1,)), ((), ())), precision=precision, preferred_element_type=jnp.float32
    )


def dot(a, b, precision=HIGHEST):
    return lax.dot_general(
        a, b, (((1,), (0,)), ((), ())), precision=precision, preferred_element_type=jnp.float32
    )


def halves(x):
    high = x.astype(jnp.bfloat16)
    return high, (x - high.astype(jnp.float32)).astype(jnp.bfloat16)


MESSAGES = (
    [("x1", dy, q) for dy in (2, 1, 3, 0) for q in (0, 1)]
    + [(ring, part) for ring in ("b1", "b0", "a0") for part in ("p1lo", "p1hi", "p2hi", "p2lo", "p3lo", "p3hi")]
    + [("x3", q) for q in (2, 3)]
)
SLOT = {key: i for i, key in enumerate(MESSAGES)}
OTHERS = [(dx, dy) for dx in (0, 1) for dy in range(4) if (dx, dy) != (0, 0)]
GATHERS = (
    [("core", dx, dy, p) for dx in (0, 1) for dy in range(4) for p in (0, 1, 2)]
    + [("corez", dx, dy) for dx, dy in OTHERS]
    + [(way, p) for way in ("y+", "y-") for p in (0, 1, 2)]
    + [(way, p) for way in ("y++", "y--") for p in (0, 1)]
    + [("x", dy, p) for dy in range(4) for p in (0, 1, 2)]
    + [(way, dx, dy) for way in ("z+", "z-") for dx, dy in OTHERS]
)
GATHER = {key: i for i, key in enumerate(GATHERS)}


def kernel(
    act_hbm, cot_hbm, mom_hbm, par_hbm, band_hbm, f_hbm, ft_hbm,
    new_w, new_m,
    act, act2, cot, mom, par, band, fm, ftm, low_parts, ft_parts, weights, g, base, column, here, out_q, in_q,
    corners, corners2, corner_out, corner_in, sent, sent_in, spread_values, coefs, low_sum,
    local_sem, act_sem, act_send, act_recv, sib_send, sib_recv, q_send, q_recv, c_send, c_recv,
    r_send, r_recv, w_send, w_recv,
):
    rep, fsdp = lax.axis_index("rep"), lax.axis_index("fsdp")
    x_hi, z = rep // 8, lax.rem(rep, 8)
    x_lo, y, core = fsdp // 8, lax.rem(fsdp // 2, 4), lax.rem(fsdp, 2)

    def chunk(dx, dy):
        return lax.rem(x_lo + dx, 2) * 4 + lax.rem(y + dy, 4)

    def shard(dx, dy, dc=0):
        return chunk(dx, dy) * 2 + lax.rem(core + dc, 2)

    def peer(dx, dy, dc=0):
        return (rep, shard(dx, dy, dc))

    def rep_peer(k):
        return (lax.rem(rep + k, N_REP), fsdp)

    x_hi_peer = (lax.rem(x_hi + 1, 2) * 8 + z, shard(1, 0))
    x_peer, up, down, sibling = peer(1, 0), peer(0, 1), peer(0, 3), peer(0, 0, 1)
    ahead = (x_hi * 8 + lax.rem(z + 1, 8), fsdp)
    behind = (x_hi * 8 + lax.rem(z + 7, 8), fsdp)

    barrier = pltpu.get_barrier_semaphore()
    greeted = [rep_peer(k) for k in range(1, N_REP)] + [x_hi_peer, sibling]
    greeted += [peer(dx, dy) for dx, dy in ORDER[:-1]]
    for other in greeted:
        pl.semaphore_signal(barrier, inc=1, device_id=other, device_id_type=MESH)

    def load(src, dst, i):
        copy = pltpu.make_async_copy(src, dst, local_sem.at[i])
        copy.start()
        return copy

    first = [load(cot_hbm, cot, 0), load(f_hbm, fm, 1), load(ft_hbm, ftm, 4)]

    def act_local(i):
        lanes = pl.ds(pl.multiple_of(i * 2 * ROWS, 2 * ROWS), 2 * ROWS)
        return pltpu.make_async_copy(act_hbm.at[:, lanes], act.at[:, lanes], act_sem.at[i])

    for i in range(8):
        act_local(i).start()
    second = [load(band_hbm, band, 2), load(mom_hbm.at[0], mom, 3), load(par_hbm, par, 5)]

    for copy in first:
        copy.wait()
    turned = cot[...].astype(jnp.float32).T.astype(jnp.bfloat16)
    weights[:, pl.ds(0, TOK)] = turned
    low = dot(jnp.concatenate(halves(fm[...]), axis=0), turned, None)
    low_parts[...] = jnp.concatenate(halves(low[:128] + low[128:]), axis=0)
    ft_parts[...] = jnp.concatenate(halves(ftm[...]), axis=1)

    def corner(i, carry):
        act_local(i).wait()
        for half in (0, 1):
            lanes = pl.ds(pl.multiple_of((i * 2 + half) * ROWS, ROWS), ROWS)
            both = dot(low_parts[...], act[:, lanes], None)
            both = jnp.concatenate(halves(both[:128] + both[128:]), axis=0)
            both = dot(both, ft_parts[...], None)
            corners[half, i] = both[:128, :128] + (both[:128, 128:] + both[128:, :128])
        return carry

    lax.fori_loop(0, 8, corner, 0)

    pl.semaphore_wait(barrier, len(greeted))

    def to_sibling(src, dst, i):
        return pltpu.make_async_remote_copy(
            src_ref=src, dst_ref=dst, send_sem=sib_send.at[i], recv_sem=sib_recv.at[i],
            device_id=sibling, device_id_type=MESH,
        )

    corner_swap = to_sibling(corners.at[1 - core], corners2, 0)
    corner_swap.start()
    weight_swap = to_sibling(weights.at[:, pl.ds(0, TOK)], weights.at[:, pl.ds(TOK, TOK)], 1)
    weight_swap.start()

    def act_copy(dx, dy):
        i = chunk(dx, dy)
        lanes = pl.ds(pl.multiple_of((i * 2 + 1 - core) * ROWS, ROWS), ROWS)
        return pltpu.make_async_remote_copy(
            src_ref=act.at[:, lanes], dst_ref=act2.at[i],
            send_sem=act_send.at[i], recv_sem=act_recv.at[i], device_id=sibling, device_id_type=MESH,
        )

    for dx, dy in ORDER:
        act_copy(dx, dy).start()

    def rows_of(q, r, p):
        return pl.ds(pl.multiple_of(q * QUARTER + r * 32, 32), 32), pl.ds(p * 128, 128)

    def peak_of(i, q):
        def body(r, peak):
            for p in range(4):
                rows, lanes = rows_of(q, r, p)
                v = jnp.abs(g[i, rows, lanes])
                peak = jnp.maximum(peak, jnp.max(v.reshape(4, 8, 128), axis=0))
            return peak

        return lax.fori_loop(0, QUARTER // 32, body, jnp.zeros((8, 128), jnp.float32))

    def unpack(key, r, p):
        slot = SLOT[key]
        rows = pl.ds(pl.multiple_of(p * QUARTER + r * 32, 32), 32)
        return in_q[slot, rows, :].astype(jnp.int32).astype(jnp.float32)

    def scale_of(code):
        return jnp.exp(code.astype(jnp.int32).astype(jnp.float32) * (1.0 / CODE)) * (1.0 / FULL)

    def received_scale(key):
        code = in_q[SLOT[key], pl.ds(4 * QUARTER, 16), :]
        return scale_of(code)[0:1]

    def add_received(i, q, keys):
        scales = [received_scale(key) for key in keys]

        def body(r, peak):
            for p in range(4):
                rows, lanes = rows_of(q, r, p)
                v = g[i, rows, lanes]
                for key, scale in zip(keys, scales, strict=True):
                    v = v + unpack(key, r, p) * scale
                g[i, rows, lanes] = v
                peak = jnp.maximum(peak, jnp.max(jnp.abs(v).reshape(4, 8, 128), axis=0))
            return peak

        return lax.fori_loop(0, QUARTER // 32, body, jnp.zeros((8, 128), jnp.float32))

    def message(key, target):
        slot = SLOT[key]
        return pltpu.make_async_remote_copy(
            src_ref=out_q.at[slot], dst_ref=in_q.at[slot], send_sem=q_send.at[slot],
            recv_sem=q_recv.at[slot], device_id=target, device_id_type=MESH,
        )

    target_of = {"p1lo": up, "p1hi": down, "p2hi": up, "p2lo": down, "p3lo": up, "p3hi": down}

    def message_of(key):
        return message(key, x_peer if key[0] in ("x1", "x3") else target_of[key[1]])

    def send(key, i, q, peak):
        slot = SLOT[key]
        peak = jnp.max(peak, axis=0, keepdims=True)
        code = jnp.broadcast_to(code_of(peak), (16, 128)).astype(jnp.int32).astype(jnp.int16)
        out_q[slot, pl.ds(4 * QUARTER, 16), :] = code
        inverse = 1.0 / scale_of(code)[0:1]

        def body(r, carry):
            for p in range(4):
                rows, lanes = rows_of(q, r, p)
                v = jnp.round(g[i, rows, lanes] * inverse).astype(jnp.int32).astype(jnp.int16)
                out_q[slot, pl.ds(pl.multiple_of(p * QUARTER + r * 32, 32), 32), :] = v
            return carry

        lax.fori_loop(0, QUARTER // 32, body, 0)
        message_of(key).start()

    def arrived(*keys):
        for key in keys:
            message_of(key).wait_recv()

    def corner_copy(dx, dy):
        k = dx * 4 + dy
        return pltpu.make_async_remote_copy(
            src_ref=corner_out.at[k], dst_ref=corner_in.at[k], send_sem=c_send.at[k],
            recv_sem=c_recv.at[k], device_id=peer(dx, dy), device_id_type=MESH,
        )

    def code_of(peak):
        return jnp.ceil(jnp.log(jnp.maximum(peak, 1e-30)) * CODE) + 1.0

    corner_swap.wait()
    for dx, dy in ORDER[:-1]:
        i = chunk(dx, dy)
        both = corners[core, i] + corners2[i]
        code = code_of(jnp.max(jnp.abs(both), axis=0, keepdims=True))
        code = jnp.broadcast_to(code, (16, 128)).astype(jnp.int32).astype(jnp.int16)
        corner_out[dx * 4 + dy, pl.ds(128, 16), :] = code
        both = jnp.round(both * (1.0 / scale_of(code)[0:1]))
        corner_out[dx * 4 + dy, pl.ds(0, 128), :] = both.astype(jnp.int32).astype(jnp.int16)
        corner_copy(dx, dy).start()
    weight_swap.wait()

    def gradient_of(dx, dy):
        i = chunk(dx, dy)
        act_copy(dx, dy).wait()

        def product(n, carry):
            lanes = pl.ds(pl.multiple_of(n * 256, 256), 256)
            own = pl.ds(pl.multiple_of((i * 2 + core) * ROWS + n * 256, 256), 256)
            g[i, :, lanes] = dot(weights[:, pl.ds(0, TOK)], act[:, own], None) + dot(
                weights[:, pl.ds(TOK, TOK)], act2[i, :, lanes], None
            )
            return carry

        lax.fori_loop(0, ROWS // 256, product, 0)
        ring = "b1" if dx else "b0"
        sends = {2: [((ring, "p1lo"), 2), ((ring, "p1hi"), 3)], 1: [((ring, "p2hi"), 3)], 3: [((ring, "p2lo"), 2)], 0: []}[dy]
        for key, q in sends:
            send(key, i, q, peak_of(i, q))

    def across(dy):
        for q in (0, 1):
            send(("x1", dy, q), chunk(1, dy), q, peak_of(chunk(1, dy), q))

    def collect(table):
        for b in range(8):
            rows = pl.ds(b * 32, 32)
            total = jnp.zeros((32, 128), jnp.float32)
            for c in range(16):
                total = total + jnp.where(column[rows, :] == c, table[b * 16 + c][None, :], 0.0)
            spread_values[rows, :] = total * here[rows, :]
        return dot_last(pick, spread_values[...])

    def scatter(values):
        spread = lax.dot_general(
            values, pick, (((0,), (0,)), ((), ())), precision=HIGHEST, preferred_element_type=jnp.float32
        )
        spread_values[...] = spread * here[...]
        wanted = lax.broadcasted_iota(jnp.int32, (16, 32, 128), 0)
        for b in range(8):
            rows = pl.ds(b * 32, 32)
            hit = jnp.where(column[rows, :][None] == wanted, spread_values[rows, :][None], 0.0)
            coefs[pl.ds(b * 16, 16), :] = jnp.sum(hit, axis=1)

    def inverse():
        return dot(dot_last(ftm[...], coefs[...]), fm[...])

    def sent_copy(k):
        return pltpu.make_async_remote_copy(
            src_ref=sent, dst_ref=sent_in.at[k], send_sem=r_send.at[k],
            recv_sem=r_recv.at[k], device_id=rep_peer(k), device_id_type=MESH,
        )

    def chunk_rows(dx, dy, first=0, count=ROWS):
        return pl.ds(pl.multiple_of(shard(dx, dy) * ROWS + first, 16), count)

    copies = {}

    def gather(key, rows, target):
        k = GATHER[key]
        copies[key] = pltpu.make_async_remote_copy(
            src_ref=new_w.at[rows], dst_ref=new_w.at[rows], send_sem=w_send.at[k],
            recv_sem=w_recv.at[k], device_id=target, device_id_type=MESH,
        )
        copies[key].start()

    lower = lax.rem(z, 2)
    mine, theirs = lower * (2 * PART + KEPT), (1 - lower) * (2 * PART + KEPT)

    def rows_of_part(dx, dy, p):
        if p == 2:
            return chunk_rows(dx, dy, 2 * PART, KEPT)
        return chunk_rows(dx, dy, mine + p * PART, PART)

    def share(dx, dy, p):
        rows = rows_of_part(dx, dy, p)
        if dx == 0:
            gather(("x", dy, p), rows, x_peer if p == 2 else x_hi_peer)
        if (dx, dy) != (0, 0):
            if p < 2:
                gather(("z-" if p else "z+", dx, dy), rows, behind if p else ahead)
            gather(("core", dx, dy, p), rows, sibling)

    def landed(*keys):
        for key in keys:
            copies[key].wait_recv()

    def got_x(dy):
        for p in (0, 1):
            landed(("x", dy, p))
            share(1, dy, p)

    def got_x_kept(dy):
        landed(("x", dy, 2))
        share(1, dy, 2)

    def got_z(dx, dy):
        landed(("z+", dx, dy), ("z-", dx, dy))
        gather(("corez", dx, dy), chunk_rows(dx, dy, theirs, 2 * PART), sibling)

    def first_y():
        landed(("y+", 0))
        gather(("y++", 0), rows_of_part(0, 3, 0), up)
        share(0, 3, 0)
        landed(("y-", 1))
        gather(("y--", 0), rows_of_part(0, 1, 1), down)
        share(0, 1, 1)

    def second_y():
        landed(("y+", 1))
        share(0, 3, 1)
        landed(("y-", 0))
        share(0, 1, 0)

    def third_y():
        landed(("y++", 0))
        share(0, 2, 0)
        landed(("y--", 0))
        share(0, 2, 1)

    def first_kept():
        landed(("y+", 2))
        gather(("y++", 1), chunk_rows(0, 3, 2 * PART, KEPT // 2), up)
        share(0, 3, 2)
        landed(("y-", 2))
        gather(("y--", 1), chunk_rows(0, 1, 2 * PART + KEPT // 2, KEPT // 2), down)
        share(0, 1, 2)

    def second_kept():
        landed(("y++", 1), ("y--", 1))
        share(0, 2, 2)

    def forward(ring, leg, dx, dy, q, *keys):
        arrived(*keys)
        send((ring, leg), chunk(dx, dy), q, add_received(chunk(dx, dy), q, keys))

    def b_second(ring, dx):
        forward(ring, "p3lo", dx, 1, 2, (ring, "p1lo"))
        forward(ring, "p3hi", dx, 3, 3, (ring, "p1hi"))

    def a_first():
        forward("a0", "p1lo", 0, 2, 0, ("x1", 2, 0))
        forward("a0", "p1hi", 0, 2, 1, ("x1", 2, 1))

    def a_direct():
        forward("a0", "p2hi", 0, 1, 1, ("x1", 1, 1))
        forward("a0", "p2lo", 0, 3, 0, ("x1", 3, 0))

    def a_second():
        forward("a0", "p3lo", 0, 1, 0, ("x1", 1, 0), ("a0", "p1lo"))
        forward("a0", "p3hi", 0, 3, 1, ("x1", 3, 1), ("a0", "p1hi"))

    def b_last():
        for q, half in ((2, "lo"), (3, "hi")):
            keys = [("b1", "p2" + half), ("b1", "p3" + half)]
            arrived(*keys)
            send(("x3", q), chunk(1, 0), q, add_received(chunk(1, 0), q, keys))

    lane = lax.broadcasted_iota(jnp.int32, (8, 128), 1)
    pick = jnp.where(lane // 16 == lax.broadcasted_iota(jnp.int32, (8, 128), 0), 1.0, 0.0)

    def prepare():
        for copy in second:
            copy.wait()
        row = lax.rem(lax.broadcasted_iota(jnp.int32, (32, 128), 1), 16)
        for b in range(8):
            places = lax.dot_general(
                band[:, b, :].astype(jnp.float32), pick, (((0,), (0,)), ((), ())),
                precision=HIGHEST, preferred_element_type=jnp.float32,
            )
            places = jnp.round(places).astype(jnp.int32)
            rows = pl.ds(b * 32, 32)
            column[rows, :] = jnp.bitwise_and(places, 63)
            here[rows, :] = jnp.where(jnp.right_shift(places, 6) == row, 1.0, 0.0)
        low_sum[...] = dot_last(fm[...], dot(fm[...], mom[...])) * beta_decay

    def band_of_replica():
        i = chunk(0, 0)
        total = low_sum[...] + (corners[core, i] + corners2[i])
        for dx, dy in ORDER[:-1]:
            k = dx * 4 + dy
            corner_copy(dx, dy).wait()
            values = corner_in[k, pl.ds(0, 128), :].astype(jnp.int32).astype(jnp.float32)
            total = total + values * scale_of(corner_in[k, pl.ds(128, 16), :])[0:1]
        sent[...] = collect(total)
        for k in range(1, N_REP):
            sent_copy(k).start()

    def new_rows():
        sent_in[0] = sent[...]
        for k in range(1, N_REP):
            sent_copy(k).wait()
        mean = sent_in[rep]
        for r in range(1, N_REP):
            mean = mean + sent_in[lax.rem(N_REP + rep - r, N_REP)]
        scatter(mean * (1.0 / N_REP))
        def update(first, count):
            local_rows = pl.ds(pl.multiple_of(first, 16), count)
            change = dot(dot_last(ftm[local_rows, :], coefs[...]), fm[...])
            new_w[chunk_rows(0, 0, first, count), :] = (par[local_rows, :] - step_size * change).astype(jnp.bfloat16)

        update(mine, PART)
        gather(("y+", 0), rows_of_part(0, 0, 0), up)
        share(0, 0, 0)
        update(mine + PART, PART)
        gather(("y-", 1), rows_of_part(0, 0, 1), down)
        gather(("y+", 1), rows_of_part(0, 0, 1), up)
        gather(("y-", 0), rows_of_part(0, 0, 0), down)
        share(0, 0, 1)

    def kept_rows():
        def update(first, count):
            local_rows = pl.ds(pl.multiple_of(first, 16), count)
            change = dot(dot_last(ftm[local_rows, :], coefs[...]), fm[...])
            new_w[chunk_rows(0, 0, first, count), :] = (par[local_rows, :] - step_size * change).astype(jnp.bfloat16)

        update(2 * PART, KEPT)
        gather(("y+", 2), rows_of_part(0, 0, 2), up)
        gather(("y-", 2), rows_of_part(0, 0, 2), down)
        share(0, 0, 2)
        update(theirs, 2 * PART)
        gather(("core", 0, 0, 0), chunk_rows(0, 0), sibling)

    def remainder():
        scatter(sent[...])
        base[...] = beta_decay * mom[...] - inverse()

    def finish(q, keys):
        arrived(*keys)
        add_received(chunk(0, 0), q, keys)
        lanes = pl.ds(q * QUARTER, QUARTER)
        new_m[0, :, lanes] = base[:, lanes] + g[chunk(0, 0), lanes, :].T

    def finish_a():
        finish(0, [("x1", 0, 0), ("a0", "p2lo"), ("a0", "p3lo")])
        finish(1, [("x1", 0, 1), ("a0", "p2hi"), ("a0", "p3hi")])

    def finish_b():
        finish(2, [("b0", "p2lo"), ("b0", "p3lo"), ("x3", 2)])
        finish(3, [("b0", "p2hi"), ("b0", "p3hi"), ("x3", 3)])

    gradient_of(*ORDER[0])
    across(2)
    gradient_of(*ORDER[1])
    prepare()
    gradient_of(*ORDER[2])
    gradient_of(*ORDER[3])
    band_of_replica()
    across(1)
    across(3)
    b_second('b1',1)
    gradient_of(*ORDER[4])
    gradient_of(*ORDER[5])
    new_rows()
    kept_rows()
    gradient_of(*ORDER[6])
    a_first()
    first_y()
    second_y()
    across(0)
    b_second('b0',0)
    got_x(0)
    third_y()
    a_direct()
    b_last()
    got_x(3)
    got_x(1)
    first_kept()
    a_second()
    got_x(2)
    second_kept()
    remainder()
    got_z(0,3)
    got_z(0,1)
    got_x_kept(0)
    gradient_of(*ORDER[7])
    finish_b()
    got_z(0,2)
    got_z(1,0)
    finish_a()
    got_x_kept(3)
    got_x_kept(1)
    got_x_kept(2)
    got_z(1,3)
    got_z(1,1)
    got_z(1,2)

    for key, copy in copies.items():
        copy.wait_send()
        if key[0] in ("core", "corez"):
            copy.wait_recv()
    for key in MESSAGES:
        message_of(key).wait_send()


def local(activations, cotangent, momentum, params, band, f, ft):
    any_space = pl.BlockSpec(memory_space=pl.ANY)
    i16, f32, bf16 = jnp.int16, jnp.float32, jnp.bfloat16
    dma = pltpu.SemaphoreType.DMA
    n = len(MESSAGES)
    return pl.pallas_call(
        kernel,
        out_shape=(
            pltpu.VMEM((16 * ROWS, COLS), bf16),
            pltpu.VMEM((1, ROWS, COLS), f32),
        ),
        in_specs=[any_space] * 7,
        out_specs=(pl.BlockSpec(memory_space=pltpu.VMEM), pl.BlockSpec(memory_space=pltpu.VMEM)),
        scratch_shapes=[
            pltpu.VMEM((TOK, 16 * ROWS), bf16),
            pltpu.VMEM((8, TOK, ROWS), bf16),
            pltpu.VMEM((TOK, COLS), bf16),
            pltpu.VMEM((ROWS, COLS), f32),
            pltpu.VMEM((ROWS, COLS), f32),
            pltpu.VMEM((8, 8, 32), jnp.int32),
            pltpu.VMEM((128, 512), f32),
            pltpu.VMEM((512, 128), f32),
            pltpu.VMEM((256, TOK), bf16),
            pltpu.VMEM((512, 256), bf16),
            pltpu.VMEM((COLS, 2 * TOK), bf16),
            pltpu.VMEM((8, COLS, ROWS), f32),
            pltpu.VMEM((ROWS, COLS), f32),
            pltpu.VMEM((256, 128), jnp.int32),
            pltpu.VMEM((256, 128), f32),
            pltpu.VMEM((n, PACKED, 128), i16),
            pltpu.VMEM((n, PACKED, 128), i16),
            pltpu.VMEM((2, 8, 128, 128), f32),
            pltpu.VMEM((8, 128, 128), f32),
            pltpu.VMEM((8, 144, 128), i16),
            pltpu.VMEM((8, 144, 128), i16),
            pltpu.VMEM((8, 256), f32),
            pltpu.VMEM((N_REP, 8, 256), f32),
            pltpu.VMEM((256, 128), f32),
            pltpu.VMEM((128, 128), f32),
            pltpu.VMEM((128, 128), f32),
            dma((6,)), dma((8,)), dma((8,)), dma((8,)), dma((2,)), dma((2,)), dma((n,)), dma((n,)), dma((8,)), dma((8,)),
            dma((N_REP,)), dma((N_REP,)), dma((len(GATHERS),)), dma((len(GATHERS),)),
        ],
        compiler_params=pltpu.CompilerParams(
            collective_id=0, has_side_effects=True, vmem_limit_bytes=48 * 2**20
        ),
    )(activations, cotangent, momentum, params, band, f, ft)


def step(activations, cotangent, momentum, params, band):
    f = band_matrix()
    return local(activations, cotangent, momentum, params, band, jnp.asarray(f), jnp.asarray(f.T.copy()))


def solution(mesh):
    return jax.shard_map(
        step,
        mesh=mesh,
        in_specs=(
            P(("rep", "fsdp"), None),
            P(("rep", "fsdp"), None),
            P("rep", "fsdp", None),
            P("fsdp", None),
            P("fsdp", None, None),
        ),
        out_specs=(P(), P("rep", "fsdp", None)),
        check_vma=False,
    )
```

```python
import jax
import jax.numpy as jnp
import numpy as np
from jax import lax
from jax.experimental import pallas as pl
from jax.experimental.pallas import tpu as pltpu
from jax.sharding import PartitionSpec as P

MESH = pl.DeviceIdType.MESH
HIGHEST = lax.Precision.HIGHEST
beta_decay = 0.9
step_size = 32.0
N_REP = 16
ROWS = 512
COLS = 512
TOK = 384
QUARTER = 128
PACKED = 4 * QUARTER + 16
CODE = 64.0
FULL = 32000.0
KEPT = 64
PART = (ROWS - KEPT) // 4

ORDER = [(1, 2), (0, 2), (1, 1), (1, 3), (0, 1), (0, 3), (1, 0), (0, 0)]


def band_matrix():
    frequency = np.arange(16)[:, None]
    position = np.arange(64)[None, :]
    scaling = np.where(frequency == 0, np.sqrt(1.0 / 64.0), np.sqrt(2.0 / 64.0))
    table = scaling * np.cos(np.pi * (2.0 * position + 1.0) * frequency / 128.0)
    return np.kron(np.eye(8), table).astype(np.float32)


def dot_last(a, b, precision=HIGHEST):
    return lax.dot_general(
        a, b, (((1,), (1,)), ((), ())), precision=precision, preferred_element_type=jnp.float32
    )


def dot(a, b, precision=HIGHEST):
    return lax.dot_general(
        a, b, (((1,), (0,)), ((), ())), precision=precision, preferred_element_type=jnp.float32
    )


def halves(x):
    high = x.astype(jnp.bfloat16)
    return high, (x - high.astype(jnp.float32)).astype(jnp.bfloat16)


MESSAGES = (
    [("x1", dy, q) for dy in (2, 1, 3, 0) for q in (0, 1)]
    + [(ring, part) for ring in ("b1", "b0", "a0") for part in ("p1lo", "p1hi", "p2hi", "p2lo", "p3lo", "p3hi")]
    + [("x3", q) for q in (2, 3)]
)
SLOT = {key: i for i, key in enumerate(MESSAGES)}
OTHERS = [(dx, dy) for dx in (0, 1) for dy in range(4) if (dx, dy) != (0, 0)]
GATHERS = (
    [("core", dx, dy) for dx in (0, 1) for dy in range(4)]
    + [("corez", dx, dy) for dx, dy in OTHERS]
    + [(way, p) for way in ("y+", "y-") for p in (0, 1, 2)]
    + [(way, p) for way in ("y++", "y--") for p in (0, 1)]
    + [("x", dy, p) for dy in range(4) for p in (0, 1, 2)]
    + [(way, dx, dy) for way in ("z+", "z-") for dx, dy in OTHERS]
)
GATHER = {key: i for i, key in enumerate(GATHERS)}


def kernel(
    act_hbm, cot_hbm, mom_hbm, par_hbm, band_hbm, f_hbm, ft_hbm,
    new_w, new_m,
    act, act2, cot, mom, par, band, fm, ftm, low_parts, ft_parts, weights, g, base, column, here, out_q, in_q,
    corners, corners2, corner_out, corner_in, sent, sent_in, spread_values, coefs, low_sum,
    local_sem, act_sem, act_send, act_recv, sib_send, sib_recv, q_send, q_recv, c_send, c_recv,
    r_send, r_recv, w_send, w_recv,
):
    rep, fsdp = lax.axis_index("rep"), lax.axis_index("fsdp")
    x_hi, z = rep // 8, lax.rem(rep, 8)
    x_lo, y, core = fsdp // 8, lax.rem(fsdp // 2, 4), lax.rem(fsdp, 2)

    def chunk(dx, dy):
        return lax.rem(x_lo + dx, 2) * 4 + lax.rem(y + dy, 4)

    def shard(dx, dy, dc=0):
        return chunk(dx, dy) * 2 + lax.rem(core + dc, 2)

    def peer(dx, dy, dc=0):
        return (rep, shard(dx, dy, dc))

    def rep_peer(k):
        return (lax.rem(rep + k, N_REP), fsdp)

    x_hi_peer = (lax.rem(x_hi + 1, 2) * 8 + z, shard(1, 0))
    x_peer, up, down, sibling = peer(1, 0), peer(0, 1), peer(0, 3), peer(0, 0, 1)
    ahead = (x_hi * 8 + lax.rem(z + 1, 8), fsdp)
    behind = (x_hi * 8 + lax.rem(z + 7, 8), fsdp)

    def load(src, dst, i):
        copy = pltpu.make_async_copy(src, dst, local_sem.at[i])
        copy.start()
        return copy

    first = [load(cot_hbm, cot, 0), load(f_hbm, fm, 1), load(ft_hbm, ftm, 4)]

    def act_local(i):
        lanes = pl.ds(pl.multiple_of(i * 2 * ROWS, 2 * ROWS), 2 * ROWS)
        return pltpu.make_async_copy(act_hbm.at[:, lanes], act.at[:, lanes], act_sem.at[i])

    for i in range(8):
        act_local(i).start()
    second = [load(band_hbm, band, 2), load(mom_hbm.at[0], mom, 3), load(par_hbm, par, 5)]

    barrier = pltpu.get_barrier_semaphore()
    greeted = [rep_peer(k) for k in range(1, N_REP)] + [x_hi_peer, sibling]
    greeted += [peer(dx, dy) for dx, dy in ORDER[:-1]]
    for other in greeted:
        pl.semaphore_signal(barrier, inc=1, device_id=other, device_id_type=MESH)

    for copy in first:
        copy.wait()
    turned = cot[...].astype(jnp.float32).T.astype(jnp.bfloat16)
    weights[:, pl.ds(0, TOK)] = turned
    low = dot(jnp.concatenate(halves(fm[...]), axis=0), turned, None)
    low_parts[...] = jnp.concatenate(halves(low[:128] + low[128:]), axis=0)
    ft_parts[...] = jnp.concatenate(halves(ftm[...]), axis=1)

    def corner(i, carry):
        act_local(i).wait()
        for half in (0, 1):
            lanes = pl.ds(pl.multiple_of((i * 2 + half) * ROWS, ROWS), ROWS)
            both = dot(low_parts[...], act[:, lanes], None)
            both = jnp.concatenate(halves(both[:128] + both[128:]), axis=0)
            both = dot(both, ft_parts[...], None)
            corners[half, i] = both[:128, :128] + (both[:128, 128:] + both[128:, :128])
        return carry

    lax.fori_loop(0, 8, corner, 0)

    pl.semaphore_wait(barrier, len(greeted))

    def to_sibling(src, dst, i):
        return pltpu.make_async_remote_copy(
            src_ref=src, dst_ref=dst, send_sem=sib_send.at[i], recv_sem=sib_recv.at[i],
            device_id=sibling, device_id_type=MESH,
        )

    corner_swap = to_sibling(corners.at[1 - core], corners2, 0)
    corner_swap.start()
    weight_swap = to_sibling(weights.at[:, pl.ds(0, TOK)], weights.at[:, pl.ds(TOK, TOK)], 1)
    weight_swap.start()

    def act_copy(dx, dy):
        i = chunk(dx, dy)
        lanes = pl.ds(pl.multiple_of((i * 2 + 1 - core) * ROWS, ROWS), ROWS)
        return pltpu.make_async_remote_copy(
            src_ref=act.at[:, lanes], dst_ref=act2.at[i],
            send_sem=act_send.at[i], recv_sem=act_recv.at[i], device_id=sibling, device_id_type=MESH,
        )

    for dx, dy in ORDER:
        act_copy(dx, dy).start()

    def rows_of(q, r, p):
        return pl.ds(pl.multiple_of(q * QUARTER + r * 32, 32), 32), pl.ds(p * 128, 128)

    def peak_of(i, q):
        def body(r, peak):
            for p in range(4):
                rows, lanes = rows_of(q, r, p)
                v = jnp.abs(g[i, rows, lanes])
                peak = jnp.maximum(peak, jnp.max(v.reshape(4, 8, 128), axis=0))
            return peak

        return lax.fori_loop(0, QUARTER // 32, body, jnp.zeros((8, 128), jnp.float32))

    def unpack(key, r, p):
        slot = SLOT[key]
        rows = pl.ds(pl.multiple_of(p * QUARTER + r * 32, 32), 32)
        return in_q[slot, rows, :].astype(jnp.int32).astype(jnp.float32)

    def scale_of(code):
        return jnp.exp(code.astype(jnp.int32).astype(jnp.float32) * (1.0 / CODE)) * (1.0 / FULL)

    def received_scale(key):
        code = in_q[SLOT[key], pl.ds(4 * QUARTER, 16), :]
        return scale_of(code)[0:1]

    def add_received(i, q, keys):
        scales = [received_scale(key) for key in keys]

        def body(r, peak):
            for p in range(4):
                rows, lanes = rows_of(q, r, p)
                v = g[i, rows, lanes]
                for key, scale in zip(keys, scales, strict=True):
                    v = v + unpack(key, r, p) * scale
                g[i, rows, lanes] = v
                peak = jnp.maximum(peak, jnp.max(jnp.abs(v).reshape(4, 8, 128), axis=0))
            return peak

        return lax.fori_loop(0, QUARTER // 32, body, jnp.zeros((8, 128), jnp.float32))

    def message(key, target):
        slot = SLOT[key]
        return pltpu.make_async_remote_copy(
            src_ref=out_q.at[slot], dst_ref=in_q.at[slot], send_sem=q_send.at[slot],
            recv_sem=q_recv.at[slot], device_id=target, device_id_type=MESH,
        )

    target_of = {"p1lo": up, "p1hi": down, "p2hi": up, "p2lo": down, "p3lo": up, "p3hi": down}

    def message_of(key):
        return message(key, x_peer if key[0] in ("x1", "x3") else target_of[key[1]])

    def send(key, i, q, peak):
        slot = SLOT[key]
        peak = jnp.max(peak, axis=0, keepdims=True)
        code = jnp.broadcast_to(code_of(peak), (16, 128)).astype(jnp.int32).astype(jnp.int16)
        out_q[slot, pl.ds(4 * QUARTER, 16), :] = code
        inverse = 1.0 / scale_of(code)[0:1]

        def body(r, carry):
            for p in range(4):
                rows, lanes = rows_of(q, r, p)
                v = jnp.round(g[i, rows, lanes] * inverse).astype(jnp.int32).astype(jnp.int16)
                out_q[slot, pl.ds(pl.multiple_of(p * QUARTER + r * 32, 32), 32), :] = v
            return carry

        lax.fori_loop(0, QUARTER // 32, body, 0)
        message_of(key).start()

    def arrived(*keys):
        for key in keys:
            message_of(key).wait_recv()

    def corner_copy(dx, dy):
        k = dx * 4 + dy
        return pltpu.make_async_remote_copy(
            src_ref=corner_out.at[k], dst_ref=corner_in.at[k], send_sem=c_send.at[k],
            recv_sem=c_recv.at[k], device_id=peer(dx, dy), device_id_type=MESH,
        )

    def code_of(peak):
        return jnp.ceil(jnp.log(jnp.maximum(peak, 1e-30)) * CODE) + 1.0

    def corners_out():
        corner_swap.wait()
        for dx, dy in ORDER[:-1]:
            i = chunk(dx, dy)
            both = corners[core, i] + corners2[i]
            code = code_of(jnp.max(jnp.abs(both), axis=0, keepdims=True))
            code = jnp.broadcast_to(code, (16, 128)).astype(jnp.int32).astype(jnp.int16)
            corner_out[dx * 4 + dy, pl.ds(128, 16), :] = code
            both = jnp.round(both * (1.0 / scale_of(code)[0:1]))
            corner_out[dx * 4 + dy, pl.ds(0, 128), :] = both.astype(jnp.int32).astype(jnp.int16)
            corner_copy(dx, dy).start()
        weight_swap.wait()

    def gradient_of(dx, dy):
        i = chunk(dx, dy)
        act_copy(dx, dy).wait()

        def product(n, carry):
            lanes = pl.ds(pl.multiple_of(n * 256, 256), 256)
            own = pl.ds(pl.multiple_of((i * 2 + core) * ROWS + n * 256, 256), 256)
            g[i, :, lanes] = dot(weights[:, pl.ds(0, TOK)], act[:, own], None) + dot(
                weights[:, pl.ds(TOK, TOK)], act2[i, :, lanes], None
            )
            return carry

        lax.fori_loop(0, ROWS // 256, product, 0)
        ring = "b1" if dx else "b0"
        sends = {2: [((ring, "p1lo"), 2), ((ring, "p1hi"), 3)], 1: [((ring, "p2hi"), 3)], 3: [((ring, "p2lo"), 2)], 0: []}[dy]
        for key, q in sends:
            send(key, i, q, peak_of(i, q))

    def across(dy):
        for q in (0, 1):
            send(("x1", dy, q), chunk(1, dy), q, peak_of(chunk(1, dy), q))

    def collect(table):
        for b in range(8):
            rows = pl.ds(b * 32, 32)
            total = jnp.zeros((32, 128), jnp.float32)
            for c in range(16):
                total = total + jnp.where(column[rows, :] == c, table[b * 16 + c][None, :], 0.0)
            spread_values[rows, :] = total * here[rows, :]
        return dot_last(pick, spread_values[...])

    def scatter(values):
        spread = lax.dot_general(
            values, pick, (((0,), (0,)), ((), ())), precision=HIGHEST, preferred_element_type=jnp.float32
        )
        spread_values[...] = spread * here[...]
        wanted = lax.broadcasted_iota(jnp.int32, (16, 32, 128), 0)
        for b in range(8):
            rows = pl.ds(b * 32, 32)
            hit = jnp.where(column[rows, :][None] == wanted, spread_values[rows, :][None], 0.0)
            coefs[pl.ds(b * 16, 16), :] = jnp.sum(hit, axis=1)

    def inverse():
        return dot(dot_last(ftm[...], coefs[...]), fm[...])

    def sent_copy(k):
        return pltpu.make_async_remote_copy(
            src_ref=sent, dst_ref=sent_in.at[k], send_sem=r_send.at[k],
            recv_sem=r_recv.at[k], device_id=rep_peer(k), device_id_type=MESH,
        )

    def chunk_rows(dx, dy, first=0, count=ROWS):
        return pl.ds(pl.multiple_of(shard(dx, dy) * ROWS + first, 16), count)

    copies = {}

    def gather(key, rows, target):
        k = GATHER[key]
        copies[key] = pltpu.make_async_remote_copy(
            src_ref=new_w.at[rows], dst_ref=new_w.at[rows], send_sem=w_send.at[k],
            recv_sem=w_recv.at[k], device_id=target, device_id_type=MESH,
        )
        copies[key].start()

    lower = lax.rem(z, 2)
    mine, theirs = lower * (2 * PART + KEPT), (1 - lower) * (2 * PART + KEPT)

    def rows_of_part(dx, dy, p):
        if p == 2:
            return chunk_rows(dx, dy, 2 * PART, KEPT)
        return chunk_rows(dx, dy, mine + p * PART, PART)

    def share(dx, dy, p):
        rows = rows_of_part(dx, dy, p)
        if dx == 0:
            gather(("x", dy, p), rows, x_peer if p == 2 else x_hi_peer)
        if (dx, dy) != (0, 0):
            if p < 2:
                gather(("z-" if p else "z+", dx, dy), rows, behind if p else ahead)

    def landed(*keys):
        for key in keys:
            copies[key].wait_recv()

    def got_x(dy):
        for p in (0, 1):
            landed(("x", dy, p))
            share(1, dy, p)

    def to_core(dx, dy):
        gather(("core", dx, dy), chunk_rows(dx, dy, lower * (2 * PART), 2 * PART + KEPT), sibling)

    def got_x_kept(dy):
        landed(("x", dy, 2))
        to_core(1, dy)

    def got_z(dx, dy):
        landed(("z+", dx, dy), ("z-", dx, dy))
        gather(("corez", dx, dy), chunk_rows(dx, dy, theirs, 2 * PART), sibling)

    def first_y():
        landed(("y+", 0))
        gather(("y++", 0), rows_of_part(0, 3, 0), up)
        share(0, 3, 0)
        landed(("y-", 1))
        gather(("y--", 0), rows_of_part(0, 1, 1), down)
        share(0, 1, 1)

    def second_y():
        landed(("y+", 1))
        share(0, 3, 1)
        landed(("y-", 0))
        share(0, 1, 0)

    def third_y():
        landed(("y++", 0))
        share(0, 2, 0)
        landed(("y--", 0))
        share(0, 2, 1)

    def first_kept():
        landed(("y+", 2))
        gather(("y++", 1), chunk_rows(0, 3, 2 * PART, KEPT // 2), up)
        share(0, 3, 2)
        to_core(0, 3)
        landed(("y-", 2))
        gather(("y--", 1), chunk_rows(0, 1, 2 * PART + KEPT // 2, KEPT // 2), down)
        share(0, 1, 2)
        to_core(0, 1)

    def second_kept():
        landed(("y++", 1), ("y--", 1))
        share(0, 2, 2)
        to_core(0, 2)

    def forward(ring, leg, dx, dy, q, *keys):
        arrived(*keys)
        send((ring, leg), chunk(dx, dy), q, add_received(chunk(dx, dy), q, keys))

    def b_second(ring, dx):
        forward(ring, "p3lo", dx, 1, 2, (ring, "p1lo"))
        forward(ring, "p3hi", dx, 3, 3, (ring, "p1hi"))

    def a_first():
        forward("a0", "p1lo", 0, 2, 0, ("x1", 2, 0))
        forward("a0", "p1hi", 0, 2, 1, ("x1", 2, 1))

    def a_direct():
        forward("a0", "p2hi", 0, 1, 1, ("x1", 1, 1))
        forward("a0", "p2lo", 0, 3, 0, ("x1", 3, 0))

    def a_second():
        forward("a0", "p3lo", 0, 1, 0, ("x1", 1, 0), ("a0", "p1lo"))
        forward("a0", "p3hi", 0, 3, 1, ("x1", 3, 1), ("a0", "p1hi"))

    def b_last():
        for q, half in ((2, "lo"), (3, "hi")):
            keys = [("b1", "p2" + half), ("b1", "p3" + half)]
            arrived(*keys)
            send(("x3", q), chunk(1, 0), q, add_received(chunk(1, 0), q, keys))

    lane = lax.broadcasted_iota(jnp.int32, (8, 128), 1)
    pick = jnp.where(lane // 16 == lax.broadcasted_iota(jnp.int32, (8, 128), 0), 1.0, 0.0)

    def prepare():
        for copy in second:
            copy.wait()
        row = lax.rem(lax.broadcasted_iota(jnp.int32, (32, 128), 1), 16)
        for b in range(8):
            places = lax.dot_general(
                band[:, b, :].astype(jnp.float32), pick, (((0,), (0,)), ((), ())),
                precision=HIGHEST, preferred_element_type=jnp.float32,
            )
            places = jnp.round(places).astype(jnp.int32)
            rows = pl.ds(b * 32, 32)
            column[rows, :] = jnp.bitwise_and(places, 63)
            here[rows, :] = jnp.where(jnp.right_shift(places, 6) == row, 1.0, 0.0)
        low_sum[...] = dot_last(fm[...], dot(fm[...], mom[...])) * beta_decay

    def band_of_replica():
        i = chunk(0, 0)
        total = low_sum[...] + (corners[core, i] + corners2[i])
        for dx, dy in ORDER[:-1]:
            k = dx * 4 + dy
            corner_copy(dx, dy).wait()
            values = corner_in[k, pl.ds(0, 128), :].astype(jnp.int32).astype(jnp.float32)
            total = total + values * scale_of(corner_in[k, pl.ds(128, 16), :])[0:1]
        sent[...] = collect(total)
        for k in (12, 4, 11, 13, 3, 5, 10, 14, 2, 6, 9, 15, 1, 7, 8):
            sent_copy(k).start()

    def new_rows():
        sent_in[0] = sent[...]
        for k in range(1, N_REP):
            sent_copy(k).wait()
        mean = sent_in[rep]
        for r in range(1, N_REP):
            mean = mean + sent_in[lax.rem(N_REP + rep - r, N_REP)]
        scatter(mean * (1.0 / N_REP))
        def update(first, count):
            local_rows = pl.ds(pl.multiple_of(first, 16), count)
            change = dot(dot_last(ftm[local_rows, :], coefs[...]), fm[...])
            new_w[chunk_rows(0, 0, first, count), :] = (par[local_rows, :] - step_size * change).astype(jnp.bfloat16)

        update(mine, PART)
        gather(("y+", 0), rows_of_part(0, 0, 0), up)
        share(0, 0, 0)
        update(mine + PART, PART)
        gather(("y-", 1), rows_of_part(0, 0, 1), down)
        gather(("y+", 1), rows_of_part(0, 0, 1), up)
        gather(("y-", 0), rows_of_part(0, 0, 0), down)
        share(0, 0, 1)

    def kept_rows():
        def update(first, count):
            local_rows = pl.ds(pl.multiple_of(first, 16), count)
            change = dot(dot_last(ftm[local_rows, :], coefs[...]), fm[...])
            new_w[chunk_rows(0, 0, first, count), :] = (par[local_rows, :] - step_size * change).astype(jnp.bfloat16)

        update(2 * PART, KEPT)
        gather(("y+", 2), rows_of_part(0, 0, 2), up)
        gather(("y-", 2), rows_of_part(0, 0, 2), down)
        share(0, 0, 2)
        update(theirs, 2 * PART)
        gather(("core", 0, 0), chunk_rows(0, 0), sibling)

    def remainder():
        scatter(sent[...])
        base[...] = beta_decay * mom[...] - inverse()

    def finish(q, keys):
        arrived(*keys)
        add_received(chunk(0, 0), q, keys)
        lanes = pl.ds(q * QUARTER, QUARTER)
        new_m[0, :, lanes] = base[:, lanes] + g[chunk(0, 0), lanes, :].T

    def finish_a():
        finish(0, [("x1", 0, 0), ("a0", "p2lo"), ("a0", "p3lo")])
        finish(1, [("x1", 0, 1), ("a0", "p2hi"), ("a0", "p3hi")])

    def finish_b():
        finish(2, [("b0", "p2lo"), ("b0", "p3lo"), ("x3", 2)])
        finish(3, [("b0", "p2hi"), ("b0", "p3hi"), ("x3", 3)])

    prepare()
    corners_out()
    gradient_of(*ORDER[0])
    gradient_of(*ORDER[1])
    gradient_of(*ORDER[2])
    gradient_of(*ORDER[3])
    band_of_replica()
    across(2)
    across(1)
    across(3)
    b_second('b1',1)
    gradient_of(*ORDER[4])
    gradient_of(*ORDER[5])
    new_rows()
    kept_rows()
    a_first()
    gradient_of(*ORDER[6])
    gradient_of(*ORDER[7])
    first_y()
    second_y()
    across(0)
    got_x(0)
    b_second('b0',0)
    third_y()
    a_direct()
    got_x(3)
    got_x(1)
    b_last()
    first_kept()
    a_second()
    got_x(2)
    second_kept()
    remainder()
    got_x_kept(0)
    got_z(0,3)
    got_z(0,1)
    finish_b()
    got_z(0,2)
    got_z(1,0)
    finish_a()
    got_x_kept(3)
    got_x_kept(1)
    got_x_kept(2)
    got_z(1,3)
    got_z(1,1)
    got_z(1,2)

    for key, copy in copies.items():
        copy.wait_send()
        if key[0] in ("core", "corez"):
            copy.wait_recv()
    for key in MESSAGES:
        message_of(key).wait_send()


def local(activations, cotangent, momentum, params, band, f, ft):
    any_space = pl.BlockSpec(memory_space=pl.ANY)
    i16, f32, bf16 = jnp.int16, jnp.float32, jnp.bfloat16
    dma = pltpu.SemaphoreType.DMA
    n = len(MESSAGES)
    return pl.pallas_call(
        kernel,
        out_shape=(
            pltpu.VMEM((16 * ROWS, COLS), bf16),
            pltpu.VMEM((1, ROWS, COLS), f32),
        ),
        in_specs=[any_space] * 7,
        out_specs=(pl.BlockSpec(memory_space=pltpu.VMEM), pl.BlockSpec(memory_space=pltpu.VMEM)),
        scratch_shapes=[
            pltpu.VMEM((TOK, 16 * ROWS), bf16),
            pltpu.VMEM((8, TOK, ROWS), bf16),
            pltpu.VMEM((TOK, COLS), bf16),
            pltpu.VMEM((ROWS, COLS), f32),
            pltpu.VMEM((ROWS, COLS), f32),
            pltpu.VMEM((8, 8, 32), jnp.int32),
            pltpu.VMEM((128, 512), f32),
            pltpu.VMEM((512, 128), f32),
            pltpu.VMEM((256, TOK), bf16),
            pltpu.VMEM((512, 256), bf16),
            pltpu.VMEM((COLS, 2 * TOK), bf16),
            pltpu.VMEM((8, COLS, ROWS), f32),
            pltpu.VMEM((ROWS, COLS), f32),
            pltpu.VMEM((256, 128), jnp.int32),
            pltpu.VMEM((256, 128), f32),
            pltpu.VMEM((n, PACKED, 128), i16),
            pltpu.VMEM((n, PACKED, 128), i16),
            pltpu.VMEM((2, 8, 128, 128), f32),
            pltpu.VMEM((8, 128, 128), f32),
            pltpu.VMEM((8, 144, 128), i16),
            pltpu.VMEM((8, 144, 128), i16),
            pltpu.VMEM((8, 256), f32),
            pltpu.VMEM((N_REP, 8, 256), f32),
            pltpu.VMEM((256, 128), f32),
            pltpu.VMEM((128, 128), f32),
            pltpu.VMEM((128, 128), f32),
            dma((6,)), dma((8,)), dma((8,)), dma((8,)), dma((2,)), dma((2,)), dma((n,)), dma((n,)), dma((8,)), dma((8,)),
            dma((N_REP,)), dma((N_REP,)), dma((len(GATHERS),)), dma((len(GATHERS),)),
        ],
        compiler_params=pltpu.CompilerParams(
            collective_id=0, has_side_effects=True, vmem_limit_bytes=48 * 2**20
        ),
    )(activations, cotangent, momentum, params, band, f, ft)


def step(activations, cotangent, momentum, params, band):
    f = band_matrix()
    return local(activations, cotangent, momentum, params, band, jnp.asarray(f), jnp.asarray(f.T.copy()))


def solution(mesh):
    return jax.shard_map(
        step,
        mesh=mesh,
        in_specs=(
            P(("rep", "fsdp"), None),
            P(("rep", "fsdp"), None),
            P("rep", "fsdp", None),
            P("fsdp", None),
            P("fsdp", None, None),
        ),
        out_specs=(P(), P("rep", "fsdp", None)),
        check_vma=False,
    )
```
